32 devices in a mesh: pool: 2 (over x), row: 8 (over z, y), col: 2 (over core).
Axes of the slice: x: 2, y: 2, z: 4, core: 2. Of those that a mesh axis runs over, the one named last changes fastest.
Arguments:
- grad_slots: bfloat16 [48, 256, 14336], P(('pool', 'row'), 'col'), parts along dimension 0, may hold values from -6 to 6
- block_owner: int32 [32], P('pool'), parts along dimension 0, may hold values from 0 to 7, as said below
- factor: bfloat16 [8192, 4096], P(('pool', 'col'), 'row'), parts along dimension 0, may hold values from -0.125 to 0.125
- pattern: int32 [16, 8], P('pool'), parts along dimension 0, may hold values from 0 to 1, as said below
Outputs:
- precond: bfloat16 [8192, 14336], P(('pool', 'col'), 'row'), parts along dimension 0
The draws below stay inside these ranges and needn't reach their ends.
There are 2 independent parts, one for each index of `pool`. The reference program is written for one: setup_inputs(seed, part) draws one part's arguments, and reference() takes and returns one part's arrays. A program takes and returns all parts, laid end to end along the dimension named above; each array names one. Nothing has to cross between parts.
Inputs may be any that keep to these rules, and one draw needn't show every extreme that they name: `block_owner`: no trainer shard holds more than 3 blocks and one holds exactly 3; a shard keeps its blocks in its first slots in increasing block order, and the other slots are unused. `pattern`: 1 on the diagonal and 0 below it.
All inputs are finite; a program needn't handle non-finite values.
Results may differ from the reference program's by a relative error of at most 0.004.
Values may be sent and summed in bfloat16 or wider, within the bound.
A program may use at most 192 MiB of HBM per device.

```python
import jax
import jax.numpy as jnp

D = 4096
F = 14336
QB = 512
CAP = 3
NQ = 8
NBLK = 16
TR = 256
SLOTS = 24
N_ROW = 8


def draw_block_owner(key, part):
    key_perm = jax.random.fold_in(key, 101)
    key_owner = jax.random.fold_in(key, 202)
    key_shuffle = jax.random.fold_in(key, 303)
    slots_all = N_ROW * CAP
    ordering = jax.random.permutation(key_perm, slots_all)
    position = jnp.argsort(ordering).astype(jnp.int32)
    full_owner = jax.random.randint(key_owner, (), 0, N_ROW)
    slot_ids = jnp.arange(slots_all, dtype=jnp.int32)
    forced = (slot_ids // CAP == full_owner) | (slot_ids == 0) | (slot_ids == (N_ROW - 1) * CAP)
    scores = jnp.where(forced, slot_ids - slots_all, position)
    chosen = jnp.argsort(scores)[:NBLK]
    owners = (chosen // CAP).astype(jnp.int32)
    shuffle = jax.random.permutation(key_shuffle, NBLK)
    return owners[shuffle].astype(jnp.int32)


def draw_pattern(key, part):
    key_bits = jax.random.fold_in(key, 404)
    coin_bits = jax.random.randint(key_bits, (NQ, NQ), 0, 2)
    row_ids = jnp.arange(NQ)[:, None]
    col_ids = jnp.arange(NQ)[None, :]
    upper_bits = jnp.where(col_ids > row_ids, coin_bits, 0)
    return jnp.where(row_ids == col_ids, 1, upper_bits).astype(jnp.int32)


def levels(rng, dims, split, low, top_value):
    factor_of, own = 1.0, jax.random.fold_in(rng, 6)
    for dim, blocks in split:
        heights = jnp.exp(jax.random.uniform(jax.random.fold_in(own, dim), (blocks,), jnp.float32, low / len(split), top_value / len(split)))
        factor_of = factor_of * jnp.repeat(heights, dims[dim] // blocks).reshape([-1 if axis == dim else 1 for axis in range(len(dims))])
    return factor_of


def centred(key, shape, spread, bound, shards=(), kind=jnp.bfloat16):
    gain = levels(key, shape, shards, -0.22, 0.18) if shards else 1.0
    array = jax.random.normal(key, shape, jnp.float32) * spread * gain
    return jnp.minimum(jnp.maximum(array, -bound), bound).astype(kind)


def setup_inputs(seed: int = 0, part: int = 0) -> dict:
    keys = jax.random.split(jax.random.key(seed), 5)
    part_keys = jax.random.split(jax.random.fold_in(keys[4], part), 5)
    grad_slots = centred(part_keys[0], (SLOTS, TR, F), 1.0, 6.0, ((0, 8), (1, 2)))
    block_owner = draw_block_owner(jax.random.fold_in(jax.random.fold_in(keys[4], part), 71), part)
    factor = centred(part_keys[2], (D, D), (D // 2) ** -0.5, 0.125, ((0, 2), (1, 8)))
    pattern = draw_pattern(jax.random.fold_in(jax.random.fold_in(keys[4], part), 71), part)
    return {"grad_slots": grad_slots, "block_owner": block_owner, "factor": factor, "pattern": pattern}


def reference(grad_slots, block_owner, factor, pattern):
    block_total = block_owner.shape[0]
    same_owner = block_owner[:, None] == block_owner[None, :]
    earlier = jnp.arange(block_total)[None, :] < jnp.arange(block_total)[:, None]
    owner_rank = jnp.sum(same_owner & earlier, axis=1).astype(jnp.int32)
    slot_of = (block_owner * CAP + owner_rank).astype(jnp.int32)
    grad = jnp.take(grad_slots, slot_of, axis=0).reshape(D, F)
    pattern_full = jnp.repeat(jnp.repeat(pattern, QB, axis=0), QB, axis=1)
    keep_mask = pattern_full == 1
    factor_used = jnp.where(keep_mask, factor, jnp.zeros_like(factor))
    rows_out = []
    for block_row in range(NQ):
        row_start = block_row * QB
        rows_out.append(jnp.dot(factor_used[row_start:row_start + QB, row_start:], grad[row_start:], preferred_element_type=jnp.float32))
    return jnp.concatenate(rows_out, axis=0).astype(jnp.bfloat16)
```

```python
import functools

import jax
import jax.numpy as jnp
from jax import lax
from jax.experimental import pallas as pl
from jax.experimental.pallas import tpu as pltpu
from jax.sharding import PartitionSpec as P

CHUNK = 256


def slots_of_blocks(block_owner, slot_cap):
    block_total = block_owner.shape[0]
    same_owner = block_owner[:, None] == block_owner[None, :]
    earlier = jnp.arange(block_total)[None, :] < jnp.arange(block_total)[:, None]
    owner_rank = jnp.sum(same_owner & earlier, axis=1)
    return (block_owner * slot_cap + owner_rank).astype(jnp.int32)


def masked_factor(factor, pattern):
    row_idx = lax.axis_index("row")
    col_idx = lax.axis_index("col")
    half_rows, piece_width = factor.shape
    block_count = pattern.shape[0]
    block_size = 2 * half_rows // block_count
    half_blocks = block_count // 2
    col_block = (row_idx * piece_width + jnp.arange(piece_width)) // block_size
    row_blocks = col_idx * half_blocks + jnp.arange(half_blocks)
    keep_mask = jnp.take(jnp.take(pattern, row_blocks, axis=0), col_block, axis=1) == 1
    shaped = factor.reshape(half_blocks, block_size, piece_width)
    return jnp.where(keep_mask[:, None, :], shaped, jnp.zeros_like(shaped)).reshape(
        half_rows, piece_width
    )


def plain_body(grad_slots, block_owner, factor, pattern):
    received = lax.all_to_all(grad_slots, "row", split_axis=2, concat_axis=0, tiled=True)
    slot_of = slots_of_blocks(block_owner, grad_slots.shape[0])
    picked = lax.map(lambda s: lax.dynamic_index_in_dim(received, s, 0, keepdims=False), slot_of)
    blocks = lax.all_gather(picked, "col", axis=1, tiled=True)
    grad_cols = blocks.reshape(-1, blocks.shape[2])
    result = jnp.dot(
        lax.all_gather(masked_factor(factor, pattern), "row", axis=1, tiled=True),
        grad_cols,
        preferred_element_type=jnp.float32,
    )
    return result.astype(jnp.bfloat16)


def kernel(n_row, chunks, slot_ref, grad_ref, fac_ref, out_ref, *scratch):
    recv = scratch[:chunks]
    full = scratch[chunks : 2 * chunks]
    (fbuf, stage, g_send, g_recv, own_sem, f_send, f_recv, f_own, s_send, s_recv, o_sem) = scratch[
        2 * chunks :
    ]
    me = lax.axis_index("row")
    col = lax.axis_index("col")
    slot_cap, half_tr, _ = grad_ref.shape
    width = chunks * CHUNK
    qb = fac_ref.shape[1]
    half_blocks = fac_ref.shape[0] // qb
    block_total = full[0].shape[0]
    per_block = block_total // n_row
    first = col * half_blocks

    barrier = pltpu.get_barrier_semaphore()
    for k in range(1, n_row):
        pl.semaphore_signal(
            barrier,
            inc=1,
            device_id={"row": lax.rem(me + k, n_row)},
            device_id_type=pl.DeviceIdType.MESH,
        )
    pl.semaphore_signal(
        barrier, inc=1, device_id={"col": 1 - col}, device_id_type=pl.DeviceIdType.MESH
    )
    pl.semaphore_wait(barrier, n_row)

    def flip(r, bit):
        return r + bit - 2 * bit * lax.rem(lax.div(r, bit), 2)

    bits = []
    bit = n_row // 2
    while bit >= 1:
        bits.append(bit)
        bit //= 2

    def f_copy(src, j, i, send_idx, partner):
        rows = pl.ds(i * qb, qb)
        return pltpu.make_async_remote_copy(
            src_ref=src,
            dst_ref=fbuf.at[j, rows, :],
            send_sem=f_send.at[send_idx],
            recv_sem=f_recv.at[j * half_blocks + i],
            device_id={"row": partner},
            device_id_type=pl.DeviceIdType.MESH,
        )

    def f_each(step, act):
        partner = flip(me, bits[step])
        base = (2**step - 1) * half_blocks
        for q in range(2**step):
            j = me
            for t in range(step):
                if (q >> t) & 1:
                    j = flip(j, bits[t])
            for i in range(half_blocks):
                act(j, i, base + q * half_blocks + i, partner, q)

    def f_start(step):
        def act(j, i, idx, partner, q):
            @pl.when(j >= first + i)
            def _():
                rows = pl.ds(i * qb, qb)
                src = fac_ref.at[rows, :] if q == 0 else fbuf.at[j, rows, :]
                f_copy(src, j, i, idx, partner).start()

        f_each(step, act)

    def f_wait_recv(step):
        def act(j, i, idx, partner, q):
            other = flip(j, bits[step])

            @pl.when(other >= first + i)
            def _():
                f_copy(fbuf.at[other, pl.ds(i * qb, qb), :], other, i, idx, partner).wait_recv()

        f_each(step, act)

    def f_wait_send(step):
        def act(j, i, idx, partner, q):
            @pl.when(j >= first + i)
            def _():
                f_copy(fbuf.at[j, pl.ds(i * qb, qb), :], j, i, idx, partner).wait_send()

        f_each(step, act)

    def g_copy(c, k):
        peer = lax.rem(me + k, n_row)
        cols = pl.ds(pl.multiple_of(peer * width + c * CHUNK, CHUNK), CHUNK)
        return pltpu.make_async_remote_copy(
            src_ref=grad_ref.at[:, :, cols],
            dst_ref=recv[c].at[pl.ds(me * slot_cap, slot_cap)],
            send_sem=g_send.at[c, k],
            recv_sem=g_recv.at[c, k],
            device_id={"row": peer},
            device_id_type=pl.DeviceIdType.MESH,
        )

    def own_copy(c):
        cols = pl.ds(pl.multiple_of(me * width + c * CHUNK, CHUNK), CHUNK)
        return pltpu.make_async_copy(
            grad_ref.at[:, :, cols],
            recv[c].at[pl.ds(me * slot_cap, slot_cap)],
            own_sem.at[c],
        )

    order = sorted(range(1, n_row), key=lambda k: abs(k - n_row // 2))

    def g_start(c):
        for k in order:
            g_copy(c, k).start()
        own_copy(c).start()

    def g_wait(c):
        for k in order:
            src = lax.rem(me + n_row - k, n_row)
            pltpu.make_async_remote_copy(
                src_ref=recv[c].at[pl.ds(src * slot_cap, slot_cap)],
                dst_ref=recv[c].at[pl.ds(src * slot_cap, slot_cap)],
                send_sem=g_send.at[c, k],
                recv_sem=g_recv.at[c, k],
                device_id={"row": src},
                device_id_type=pl.DeviceIdType.MESH,
            ).wait_recv()
        own_copy(c).wait()

    half = pl.ds(pl.multiple_of(col * half_tr, half_tr), half_tr)

    def s_copy(c):
        return pltpu.make_async_remote_copy(
            src_ref=full[c].at[:, half, :],
            dst_ref=full[c].at[:, half, :],
            send_sem=s_send.at[c],
            recv_sem=s_recv.at[c],
            device_id={"col": 1 - col},
            device_id_type=pl.DeviceIdType.MESH,
        )

    def pick(c):
        def body(b, carry):
            full[c][b, half, :] = recv[c][slot_ref[b]]
            return carry

        lax.fori_loop(0, block_total, body, 0)

    def o_copy(c):
        return pltpu.make_async_copy(
            stage.at[c % 2], out_ref.at[:, pl.ds(c * CHUNK, CHUNK)], o_sem.at[c % 2]
        )

    def compute(c):
        s_copy(c).wait_recv()
        if c >= 2:
            o_copy(c - 2).wait()

        def rows_body(i, carry):
            rows = pl.ds(pl.multiple_of(i * qb, qb), qb)

            def dot_body(j, acc):
                g = full[c][pl.ds(j * per_block, per_block)].reshape(qb, CHUNK)
                return acc + jnp.dot(fbuf[j, rows, :], g, preferred_element_type=jnp.float32)

            acc = lax.fori_loop(first + i, n_row, dot_body, jnp.zeros((qb, CHUNK), jnp.float32))
            stage[c % 2, rows, :] = acc.astype(jnp.bfloat16)
            return carry

        lax.fori_loop(0, half_blocks, rows_body, 0)
        o_copy(c).start()

    fown_copy = pltpu.make_async_copy(fac_ref, fbuf.at[me], f_own)
    f_start(0)
    g_start(0)
    fown_copy.start()
    started = 1
    for step in range(len(bits)):
        if started < chunks:
            g_start(started)
            started += 1
        f_wait_recv(step)
        if step + 1 < len(bits):
            f_start(step + 1)
    fown_copy.wait()
    while started < chunks:
        g_start(started)
        started += 1
    for c in range(chunks):
        g_wait(c)
        pick(c)
        s_copy(c).start()
        if c >= 1:
            compute(c - 1)
    compute(chunks - 1)
    for c in range(chunks):
        for k in order:
            g_copy(c, k).wait_send()
        s_copy(c).wait_send()
    for step in range(len(bits)):
        f_wait_send(step)
    for c in range(max(chunks - 2, 0), chunks):
        o_copy(c).wait()


def kernel_body(n_row, grad_slots, block_owner, factor, pattern):
    slot_cap, half_tr, total_width = grad_slots.shape
    chunks = total_width // n_row // CHUNK
    half_rows, qb = factor.shape
    half_blocks = half_rows // qb
    block_total = block_owner.shape[0]
    slot_of = slots_of_blocks(block_owner, slot_cap)
    masked = masked_factor(factor, pattern)
    dma = pltpu.SemaphoreType.DMA
    return pl.pallas_call(
        functools.partial(kernel, n_row, chunks),
        out_shape=jax.ShapeDtypeStruct((half_rows, chunks * CHUNK), jnp.bfloat16),
        in_specs=[
            pl.BlockSpec(memory_space=pltpu.SMEM),
            pl.BlockSpec(memory_space=pl.ANY),
            pl.BlockSpec(memory_space=pl.ANY),
        ],
        out_specs=pl.BlockSpec(memory_space=pl.ANY),
        scratch_shapes=[pltpu.VMEM((n_row * slot_cap, half_tr, CHUNK), jnp.bfloat16)] * chunks
        + [pltpu.VMEM((block_total, 2 * half_tr, CHUNK), jnp.bfloat16)] * chunks
        + [
            pltpu.VMEM((n_row, half_rows, qb), jnp.bfloat16),
            pltpu.VMEM((2, half_rows, CHUNK), jnp.bfloat16),
            dma((chunks, n_row)),
            dma((chunks, n_row)),
            dma((chunks,)),
            dma(((n_row - 1) * half_blocks,)),
            dma((n_row * half_blocks,)),
            dma,
            dma((chunks,)),
            dma((chunks,)),
            dma((2,)),
        ],
        compiler_params=pltpu.CompilerParams(
            collective_id=0, has_side_effects=True, vmem_limit_bytes=58 * 2**20
        ),
        cost_estimate=pl.CostEstimate(
            flops=2 * half_rows * n_row * qb * chunks * CHUNK,
            bytes_accessed=4 * half_rows * chunks * CHUNK,
            transcendentals=0,
        ),
    )(slot_of, grad_slots, masked)


def solution(mesh):
    placed = (
        P(("pool", "row"), "col", None),
        P("pool"),
        P(("pool", "col"), "row"),
        P("pool", None),
    )
    n_row = mesh.shape["row"]

    def body(grad_slots, block_owner, factor, pattern):
        width = grad_slots.shape[2] // n_row
        half_tr = grad_slots.shape[1]
        one_block = factor.shape[1] * pattern.shape[0] == 2 * factor.shape[0]
        power = n_row & (n_row - 1) == 0
        whole = (block_owner.shape[0] * 2 * half_tr) % (n_row * 2 * half_tr) == 0
        tiled = width % CHUNK == 0 and half_tr % 16 == 0 and pattern.shape[0] == n_row
        if one_block and power and whole and tiled:
            return kernel_body(n_row, grad_slots, block_owner, factor, pattern)
        return plain_body(grad_slots, block_owner, factor, pattern)

    return jax.shard_map(
        body, mesh=mesh, in_specs=placed, out_specs=P(("pool", "col"), "row"), check_vma=False
    )
```

```python
import functools

import jax
import jax.numpy as jnp
from jax import lax
from jax.experimental import pallas as pl
from jax.experimental.pallas import tpu as pltpu
from jax.sharding import PartitionSpec as P

CHUNK = 256


def slots_of_blocks(block_owner, slot_cap):
    block_total = block_owner.shape[0]
    same_owner = block_owner[:, None] == block_owner[None, :]
    earlier = jnp.arange(block_total)[None, :] < jnp.arange(block_total)[:, None]
    owner_rank = jnp.sum(same_owner & earlier, axis=1)
    return (block_owner * slot_cap + owner_rank).astype(jnp.int32)


def masked_factor(factor, pattern):
    row_idx = lax.axis_index("row")
    col_idx = lax.axis_index("col")
    half_rows, piece_width = factor.shape
    block_count = pattern.shape[0]
    block_size = 2 * half_rows // block_count
    half_blocks = block_count // 2
    col_block = (row_idx * piece_width + jnp.arange(piece_width)) // block_size
    row_blocks = col_idx * half_blocks + jnp.arange(half_blocks)
    keep_mask = jnp.take(jnp.take(pattern, row_blocks, axis=0), col_block, axis=1) == 1
    shaped = factor.reshape(half_blocks, block_size, piece_width)
    return jnp.where(keep_mask[:, None, :], shaped, jnp.zeros_like(shaped)).reshape(
        half_rows, piece_width
    )


def plain_body(grad_slots, block_owner, factor, pattern):
    received = lax.all_to_all(grad_slots, "row", split_axis=2, concat_axis=0, tiled=True)
    slot_of = slots_of_blocks(block_owner, grad_slots.shape[0])
    picked = lax.map(lambda s: lax.dynamic_index_in_dim(received, s, 0, keepdims=False), slot_of)
    blocks = lax.all_gather(picked, "col", axis=1, tiled=True)
    grad_cols = blocks.reshape(-1, blocks.shape[2])
    result = jnp.dot(
        lax.all_gather(masked_factor(factor, pattern), "row", axis=1, tiled=True),
        grad_cols,
        preferred_element_type=jnp.float32,
    )
    return result.astype(jnp.bfloat16)


def kernel(n_row, chunks, slot_ref, grad_ref, fac_ref, out_ref, *scratch):
    recv = scratch[:chunks]
    full = scratch[chunks : 2 * chunks]
    (fbuf, stage, g_send, g_recv, own_sem, f_send, f_recv, f_own, s_send, s_recv, o_sem) = scratch[
        2 * chunks :
    ]
    me = lax.axis_index("row")
    col = lax.axis_index("col")
    slot_cap, half_tr, _ = grad_ref.shape
    width = chunks * CHUNK
    qb = fac_ref.shape[1]
    half_blocks = fac_ref.shape[0] // qb
    block_total = full[0].shape[0]
    per_block = block_total // n_row
    first = col * half_blocks

    barrier = pltpu.get_barrier_semaphore()
    for k in range(1, n_row):
        pl.semaphore_signal(
            barrier,
            inc=1,
            device_id={"row": lax.rem(me + k, n_row)},
            device_id_type=pl.DeviceIdType.MESH,
        )
    pl.semaphore_signal(
        barrier, inc=1, device_id={"col": 1 - col}, device_id_type=pl.DeviceIdType.MESH
    )
    pl.semaphore_wait(barrier, n_row)

    def flip(r, bit):
        return r + bit - 2 * bit * lax.rem(lax.div(r, bit), 2)

    bits = []
    bit = n_row // 2
    while bit >= 1:
        bits.append(bit)
        bit //= 2

    def f_copy(src, j, i, send_idx, partner):
        rows = pl.ds(i * qb, qb)
        return pltpu.make_async_remote_copy(
            src_ref=src,
            dst_ref=fbuf.at[j, rows, :],
            send_sem=f_send.at[send_idx],
            recv_sem=f_recv.at[j * half_blocks + i],
            device_id={"row": partner},
            device_id_type=pl.DeviceIdType.MESH,
        )

    def f_each(step, act):
        partner = flip(me, bits[step])
        base = (2**step - 1) * half_blocks
        for q in range(2**step):
            j = me
            for t in range(step):
                if (q >> t) & 1:
                    j = flip(j, bits[t])
            for i in range(half_blocks):
                act(j, i, base + q * half_blocks + i, partner, q)

    def f_start(step):
        def act(j, i, idx, partner, q):
            @pl.when(j >= first + i)
            def _():
                rows = pl.ds(i * qb, qb)
                src = fac_ref.at[rows, :] if q == 0 else fbuf.at[j, rows, :]
                f_copy(src, j, i, idx, partner).start()

        f_each(step, act)

    def f_wait_recv(step):
        def act(j, i, idx, partner, q):
            other = flip(j, bits[step])

            @pl.when(other >= first + i)
            def _():
                f_copy(fbuf.at[other, pl.ds(i * qb, qb), :], other, i, idx, partner).wait_recv()

        f_each(step, act)

    def f_wait_send(step):
        def act(j, i, idx, partner, q):
            @pl.when(j >= first + i)
            def _():
                f_copy(fbuf.at[j, pl.ds(i * qb, qb), :], j, i, idx, partner).wait_send()

        f_each(step, act)

    def g_copy(c, k):
        peer = lax.rem(me + k, n_row)
        cols = pl.ds(pl.multiple_of(peer * width + c * CHUNK, CHUNK), CHUNK)
        return pltpu.make_async_remote_copy(
            src_ref=grad_ref.at[:, :, cols],
            dst_ref=recv[c].at[pl.ds(me * slot_cap, slot_cap)],
            send_sem=g_send.at[c, k],
            recv_sem=g_recv.at[c, k],
            device_id={"row": peer},
            device_id_type=pl.DeviceIdType.MESH,
        )

    def own_copy(c):
        cols = pl.ds(pl.multiple_of(me * width + c * CHUNK, CHUNK), CHUNK)
        return pltpu.make_async_copy(
            grad_ref.at[:, :, cols],
            recv[c].at[pl.ds(me * slot_cap, slot_cap)],
            own_sem.at[c],
        )

    by_reach = sorted(range(1, n_row), key=lambda k: abs(k - n_row // 2))
    order = [by_reach[t // 2 if t % 2 == 0 else n_row - 2 - t // 2] for t in range(n_row - 1)]

    def g_start(c):
        for t in range(n_row - 1):
            near, far = order[t], order[(t + 1) % (n_row - 1)]
            g_copy(c, near + col * (far - near)).start()
        own_copy(c).start()

    def g_wait(c):
        for k in order:
            src = lax.rem(me + n_row - k, n_row)
            pltpu.make_async_remote_copy(
                src_ref=recv[c].at[pl.ds(src * slot_cap, slot_cap)],
                dst_ref=recv[c].at[pl.ds(src * slot_cap, slot_cap)],
                send_sem=g_send.at[c, k],
                recv_sem=g_recv.at[c, k],
                device_id={"row": src},
                device_id_type=pl.DeviceIdType.MESH,
            ).wait_recv()
        own_copy(c).wait()

    half = pl.ds(pl.multiple_of(col * half_tr, half_tr), half_tr)

    def s_copy(c):
        return pltpu.make_async_remote_copy(
            src_ref=full[c].at[:, half, :],
            dst_ref=full[c].at[:, half, :],
            send_sem=s_send.at[c],
            recv_sem=s_recv.at[c],
            device_id={"col": 1 - col},
            device_id_type=pl.DeviceIdType.MESH,
        )

    def pick(c):
        def body(b, carry):
            full[c][b, half, :] = recv[c][slot_ref[b]]
            return carry

        lax.fori_loop(0, block_total, body, 0)

    def o_copy(c):
        return pltpu.make_async_copy(
            stage.at[c % 2], out_ref.at[:, pl.ds(c * CHUNK, CHUNK)], o_sem.at[c % 2]
        )

    def compute(c):
        s_copy(c).wait_recv()
        if c >= 2:
            o_copy(c - 2).wait()

        def rows_body(i, carry):
            rows = pl.ds(pl.multiple_of(i * qb, qb), qb)

            def dot_body(j, acc):
                g = full[c][pl.ds(j * per_block, per_block)].reshape(qb, CHUNK)
                return acc + jnp.dot(fbuf[j, rows, :], g, preferred_element_type=jnp.float32)

            acc = lax.fori_loop(first + i, n_row, dot_body, jnp.zeros((qb, CHUNK), jnp.float32))
            stage[c % 2, rows, :] = acc.astype(jnp.bfloat16)
            return carry

        lax.fori_loop(0, half_blocks, rows_body, 0)
        o_copy(c).start()

    fown_copy = pltpu.make_async_copy(fac_ref, fbuf.at[me], f_own)
    def g_start_on(which, c):
        @pl.when(col == which)
        def _():
            g_start(c)

    f_start(0)
    g_start_on(0, 0)
    for c in range(min(4, chunks)):
        g_start_on(1, c)
    fown_copy.start()
    started = 1
    for step in range(len(bits)):
        if started < chunks:
            g_start_on(0, started)
            started += 1
        f_wait_recv(step)
        if step + 1 < len(bits):
            f_start(step + 1)
    fown_copy.wait()
    for c in range(min(4, chunks), chunks):
        g_start_on(1, c)
    while started < chunks:
        g_start_on(0, started)
        started += 1
    for c in range(chunks):
        g_wait(c)
        pick(c)
        s_copy(c).start()
        if c >= 1:
            compute(c - 1)
    compute(chunks - 1)
    for c in range(chunks):
        for k in order:
            g_copy(c, k).wait_send()
        s_copy(c).wait_send()
    for step in range(len(bits)):
        f_wait_send(step)
    for c in range(max(chunks - 2, 0), chunks):
        o_copy(c).wait()


def kernel_body(n_row, grad_slots, block_owner, factor, pattern):
    slot_cap, half_tr, total_width = grad_slots.shape
    chunks = total_width // n_row // CHUNK
    half_rows, qb = factor.shape
    half_blocks = half_rows // qb
    block_total = block_owner.shape[0]
    slot_of = slots_of_blocks(block_owner, slot_cap)
    masked = masked_factor(factor, pattern)
    dma = pltpu.SemaphoreType.DMA
    return pl.pallas_call(
        functools.partial(kernel, n_row, chunks),
        out_shape=jax.ShapeDtypeStruct((half_rows, chunks * CHUNK), jnp.bfloat16),
        in_specs=[
            pl.BlockSpec(memory_space=pltpu.SMEM),
            pl.BlockSpec(memory_space=pl.ANY),
            pl.BlockSpec(memory_space=pl.ANY),
        ],
        out_specs=pl.BlockSpec(memory_space=pl.ANY),
        scratch_shapes=[pltpu.VMEM((n_row * slot_cap, half_tr, CHUNK), jnp.bfloat16)] * chunks
        + [pltpu.VMEM((block_total, 2 * half_tr, CHUNK), jnp.bfloat16)] * chunks
        + [
            pltpu.VMEM((n_row, half_rows, qb), jnp.bfloat16),
            pltpu.VMEM((2, half_rows, CHUNK), jnp.bfloat16),
            dma((chunks, n_row)),
            dma((chunks, n_row)),
            dma((chunks,)),
            dma(((n_row - 1) * half_blocks,)),
            dma((n_row * half_blocks,)),
            dma,
            dma((chunks,)),
            dma((chunks,)),
            dma((2,)),
        ],
        compiler_params=pltpu.CompilerParams(
            collective_id=0, has_side_effects=True, vmem_limit_bytes=58 * 2**20
        ),
        cost_estimate=pl.CostEstimate(
            flops=2 * half_rows * n_row * qb * chunks * CHUNK,
            bytes_accessed=4 * half_rows * chunks * CHUNK,
            transcendentals=0,
        ),
    )(slot_of, grad_slots, masked)


def solution(mesh):
    placed = (
        P(("pool", "row"), "col", None),
        P("pool"),
        P(("pool", "col"), "row"),
        P("pool", None),
    )
    n_row = mesh.shape["row"]

    def body(grad_slots, block_owner, factor, pattern):
        width = grad_slots.shape[2] // n_row
        half_tr = grad_slots.shape[1]
        one_block = factor.shape[1] * pattern.shape[0] == 2 * factor.shape[0]
        power = n_row & (n_row - 1) == 0
        whole = (block_owner.shape[0] * 2 * half_tr) % (n_row * 2 * half_tr) == 0
        tiled = width % CHUNK == 0 and half_tr % 16 == 0 and pattern.shape[0] == n_row
        if one_block and power and whole and tiled:
            return kernel_body(n_row, grad_slots, block_owner, factor, pattern)
        return plain_body(grad_slots, block_owner, factor, pattern)

    return jax.shard_map(
        body, mesh=mesh, in_specs=placed, out_specs=P(("pool", "col"), "row"), check_vma=False
    )
```
